1024 devices in a mesh: sec: 128 (over y, z, core), mpo: 8 (over x).
Axes of the slice: x: 8, y: 8, z: 8, core: 2. Of those that a mesh axis runs over, the one named last changes fastest.
Arguments:
- wavefunction: float32 [256, 256, 256], P('sec'), may hold values from -6 to 6
- sector_sizes: int32 [256, 2], P('sec'), may hold values from 128 to 256, as said below
- left_env: float32 [24, 256, 256, 256], P('mpo', 'sec'), may hold values from -0.375 to 0.375
- right_env: float32 [24, 256, 256, 256], P('mpo', 'sec'), may hold values from -0.375 to 0.375
- mpo_coeffs: float32 [24, 256], P('mpo', 'sec'), may hold values from -4 to 4
- source_block: int32 [24, 256], P('mpo', 'sec'), may hold values from 0 to 255, as said below
Outputs:
- applied: float32 [256, 256, 256], P('sec', 'mpo')
The draws below stay inside these ranges and needn't reach their ends.
Inputs may be any that keep to these rules, and one draw needn't show every extreme that they name: source_block[w, k] lies in the index-of-sec group of block k or in the group just below or just above it, groups being runs of 2 blocks. `sector_sizes`: each entry is a multiple of 128.
All inputs are finite; a program needn't handle non-finite values.
Results may differ from the reference program's by a relative error of at most 0.0001.
Values sent between devices are 32-bit elements; how exact they have to be, the bound alone decides.
No kernel may reach another device: no remote copies, remote signals or barrier semaphores. Data moves between devices by JAX's collectives and lax.ppermute only.
A program may use at most 32 MiB of HBM per device.

```python
import jax
import jax.numpy as jnp
from jax import lax

SB = 256
GRAIN = 128
W = 24
BLK_DEV = 2
SECTORS = 256


def draw_source_block(key, part):
    key = jax.random.fold_in(key, 11)
    offset_key, within_key = jax.random.split(key)
    group_count = SECTORS // BLK_DEV
    offset_seed = jax.random.randint(offset_key, (SECTORS,), 0, 3)
    mpo_index = jnp.arange(W, dtype=jnp.int32)[:, None]
    block_index = jnp.arange(SECTORS, dtype=jnp.int32)[None, :]
    own_group = block_index // BLK_DEV
    offset = (mpo_index + offset_seed[None, :]) % 3 - 1
    target_group = jnp.clip(own_group + offset, 0, group_count - 1)
    within = jax.random.randint(within_key, (W, SECTORS), 0, BLK_DEV)
    result = (target_group * BLK_DEV + within).astype(jnp.int32)
    result = result.at[0, 0].set(0)
    result = result.at[0, SECTORS - 1].set(SECTORS - 1)
    return result


def draw_sector_sizes(key, part):
    key = jax.random.fold_in(key, 23)
    units = jax.random.randint(key, (SECTORS, 2), 1, SB // GRAIN + 1)
    result = (units * GRAIN).astype(jnp.int32)
    result = result.at[0].set(SB)
    result = result.at[1].set(GRAIN)
    return result


def block_scale(own_key, extent, pieces, low, high):
    factor_of, own = 1.0, jax.random.fold_in(own_key, 6)
    for dim, parts in pieces:
        steps = jnp.exp(jax.random.uniform(jax.random.fold_in(own, dim), (parts,), jnp.float32, low / len(pieces), high / len(pieces)))
        factor_of = factor_of * jnp.repeat(steps, extent[dim] // parts).reshape([-1 if axis == dim else 1 for axis in range(len(extent))])
    return factor_of


def gaussian(stream_key, extent, scale, bound, cuts=(), held_as=jnp.bfloat16):
    level = block_scale(stream_key, extent, cuts, -0.22, 0.18) if cuts else 1.0
    drawn = jax.random.normal(stream_key, extent, jnp.float32) * scale * level
    return jnp.minimum(jnp.maximum(drawn, -bound), bound).astype(held_as)


def setup_inputs(seed: int = 0) -> dict:
    keys = jax.random.split(jax.random.key(seed), 7)
    wavefunction = gaussian(keys[0], (SECTORS, SB, SB), 1.0, 6.0, ((0, 128),), jnp.float32)
    sector_sizes = draw_sector_sizes(jax.random.fold_in(keys[6], 71), 0)
    left_env = gaussian(keys[2], (W, SECTORS, SB, SB), SB ** -0.5, 0.375, ((0, 8), (1, 128)), jnp.float32)
    right_env = gaussian(keys[3], (W, SECTORS, SB, SB), SB ** -0.5, 0.375, ((0, 8), (1, 128)), jnp.float32)
    mpo_coeffs = gaussian(keys[4], (W, SECTORS), 0.3, 4.0, ((0, 8), (1, 128)), jnp.float32)
    source_block = draw_source_block(jax.random.fold_in(keys[6], 71), 0)
    return {"wavefunction": wavefunction, "sector_sizes": sector_sizes, "left_env": left_env, "right_env": right_env, "mpo_coeffs": mpo_coeffs, "source_block": source_block}


def reference(wavefunction, sector_sizes, left_env, right_env, mpo_coeffs, source_block):
    row_index = jnp.arange(SB, dtype=jnp.int32)
    keep_mask = (row_index[None, :, None] < sector_sizes[:, 0][:, None, None]) & (row_index[None, None, :] < sector_sizes[:, 1][:, None, None])
    masked = jnp.where(keep_mask, wavefunction, jnp.zeros_like(wavefunction))

    def accumulate(total, per_term):
        left_term, right_term, coeff_term, source_term = per_term
        chosen = masked[source_term] * coeff_term[:, None, None]
        left_done = jnp.einsum("kab,kbc->kac", left_term, chosen, precision=lax.Precision.HIGHEST)
        return total + jnp.einsum("kac,kdc->kad", left_done, right_term, precision=lax.Precision.HIGHEST), None

    total, unused = lax.scan(accumulate, jnp.zeros_like(masked), (left_env, right_env, mpo_coeffs, source_block))
    return jnp.where(keep_mask, total, jnp.zeros_like(total))
```

```python
import functools

import jax
import jax.numpy as jnp
from jax import lax
from jax.experimental import pallas as pl
from jax.experimental.pallas import tpu as pltpu
from jax.sharding import PartitionSpec as P

VMEM_LIMIT = 48 * 1024 * 1024
vmem = pl.BlockSpec(memory_space=pltpu.VMEM)
smem = pl.BlockSpec(memory_space=pltpu.SMEM)


def keep(sizes_ref, k, shape):
    rows = lax.broadcasted_iota(jnp.int32, shape, 0) < sizes_ref[k, 0]
    columns = lax.broadcasted_iota(jnp.int32, shape, 1) < sizes_ref[k, 1]
    return rows & columns


def split(value):
    high = value.astype(jnp.bfloat16)
    return high, (value - high.astype(jnp.float32)).astype(jnp.bfloat16)


def product(left, right, contract):
    dot = functools.partial(
        lax.dot_general,
        dimension_numbers=(((1,), (contract,)), ((), ())),
        preferred_element_type=jnp.float32,
    )
    (left_high, left_low), (right_high, right_low) = left, right
    return dot(left_high, right_high) + (dot(left_high, right_low) + dot(left_low, right_high))


def mask_kernel(sizes_ref, wave_ref, masked_ref):
    blocks, rows, columns = wave_ref.shape
    for k in range(blocks):
        masked_ref[k] = jnp.where(keep(sizes_ref, k, (rows, columns)), wave_ref[k], 0.0)


def near_kernel(
    sizes_ref, coeff_ref, source_ref, own_ref, after_ref, left_ref, right_ref,
    total_ref, left_high, left_low, right_high, right_low,
):
    terms, blocks, rows, columns = left_ref.shape
    parts, _, part, _ = total_ref.shape
    first = lax.axis_index("sec") * blocks
    for k in range(blocks):
        total_ref[:, k] = jnp.zeros((parts, part, columns), jnp.float32)
        for w in range(terms):
            place = source_ref[k, w] - first

            @pl.when(place >= 0)
            def _():
                own = own_ref[jnp.clip(place, 0, blocks - 1)]
                after = after_ref[jnp.clip(place - blocks, 0, blocks - 1)]
                chosen = jnp.where(place < blocks, own, after) * coeff_ref[k, w]
                done = product(split(left_ref[w, k]), split(chosen), 0)
                term = product(split(done), split(right_ref[w, k]), 1)
                term = jnp.where(keep(sizes_ref, k, (rows, columns)), term, 0.0)
                total_ref[:, k] += term.reshape(parts, part, columns)

            @pl.when(place < 0)
            def _():
                high, low = split(left_ref[w, k])
                left_high[w, k] = high
                left_low[w, k] = low
                high, low = split(right_ref[w, k])
                right_high[w, k] = high
                right_low[w, k] = low


def far_kernel(
    sizes_ref, coeff_ref, source_ref, before_ref,
    left_high, left_low, right_high, right_low, sum_ref, total_ref,
):
    terms, blocks, rows, columns = left_high.shape
    parts, _, part, _ = total_ref.shape
    total_ref[...] = sum_ref[...]
    first = lax.axis_index("sec") * blocks
    for k in range(blocks):
        for w in range(terms):
            place = source_ref[k, w] - first

            @pl.when(place < 0)
            def _():
                chosen = before_ref[jnp.clip(place + blocks, 0, blocks - 1)] * coeff_ref[k, w]
                done = product((left_high[w, k], left_low[w, k]), split(chosen), 0)
                term = product(split(done), (right_high[w, k], right_low[w, k]), 1)
                term = jnp.where(keep(sizes_ref, k, (rows, columns)), term, 0.0)
                total_ref[:, k] += term.reshape(parts, part, columns)


def on_device(wavefunction, sector_sizes, left_env, right_env, mpo_coeffs, source_block):
    blocks, rows, columns = wavefunction.shape
    terms = left_env.shape[0]
    devices, parts = lax.axis_size("sec"), lax.axis_size("mpo")
    coeffs, sources = mpo_coeffs.T, source_block.T
    params = pltpu.CompilerParams(vmem_limit_bytes=VMEM_LIMIT)
    f32 = jax.ShapeDtypeStruct((parts, blocks, rows // parts, columns), jnp.float32)
    bf16 = jax.ShapeDtypeStruct((terms, blocks, rows, columns), jnp.bfloat16)

    masked = pl.pallas_call(
        mask_kernel,
        out_shape=jax.ShapeDtypeStruct(wavefunction.shape, jnp.float32),
        in_specs=[smem, vmem],
        out_specs=vmem,
        name="mask",
    )(sector_sizes, wavefunction)

    after = lax.ppermute(masked, "sec", [(i + 1, i) for i in range(devices - 1)])
    before = lax.ppermute(masked, "sec", [(i, i + 1) for i in range(devices - 1)])

    total, *halves = pl.pallas_call(
        near_kernel,
        out_shape=[f32] + [bf16] * 4,
        in_specs=[smem] * 3 + [vmem] * 4,
        out_specs=[vmem] * 5,
        compiler_params=params,
        cost_estimate=pl.CostEstimate(
            flops=12 * 3 * 2 * rows**3, bytes_accessed=8 * 2**20, transcendentals=0
        ),
        name="near_terms",
    )(sector_sizes, coeffs, sources, masked, after, left_env, right_env)

    total = pl.pallas_call(
        far_kernel,
        out_shape=f32,
        in_specs=[smem] * 3 + [vmem] * 6,
        out_specs=vmem,
        compiler_params=params,
        cost_estimate=pl.CostEstimate(
            flops=4 * 3 * 2 * rows**3, bytes_accessed=4 * 2**20, transcendentals=0
        ),
        name="far_terms",
    )(sector_sizes, coeffs, sources, before, *halves, total)

    shares = lax.all_to_all(total, "mpo", split_axis=0, concat_axis=0, tiled=True)
    return shares.sum(0)


def solution(mesh):
    in_specs = (
        P("sec", None, None),
        P("sec", None),
        P("mpo", "sec", None, None),
        P("mpo", "sec", None, None),
        P("mpo", "sec"),
        P("mpo", "sec"),
    )
    out_specs = P("sec", "mpo", None)
    return jax.shard_map(
        on_device, mesh=mesh, in_specs=in_specs, out_specs=out_specs, check_vma=False
    )
```

```python
import functools

import jax
import jax.numpy as jnp
from jax import lax
from jax.experimental import pallas as pl
from jax.experimental.pallas import tpu as pltpu
from jax.sharding import PartitionSpec as P

VMEM_LIMIT = 40 * 1024 * 1024
vmem = pl.BlockSpec(memory_space=pltpu.VMEM)
smem = pl.BlockSpec(memory_space=pltpu.SMEM)
hbm = pl.BlockSpec(memory_space=pltpu.HBM)


def inside(limit, shape, dim):
    return lax.broadcasted_iota(jnp.int32, shape, dim) < limit


def split(value):
    high = value.astype(jnp.bfloat16)
    return high, (value - high.astype(jnp.float32)).astype(jnp.bfloat16)


def product(left, right, contract):
    (left_high, left_low), (right_high, right_low) = left, right
    return lax.dot_general(
        jnp.concatenate([left_high, left_low, left_high], axis=1),
        jnp.concatenate([right_high, right_high, right_low], axis=contract),
        dimension_numbers=(((1,), (contract,)), ((), ())),
        preferred_element_type=jnp.float32,
    )


def mask_kernel(sizes_hbm, wave_hbm, masked_ref, sizes_ref, wave_ref, small, large):
    blocks, rows, columns = wave_ref.shape
    shape = (rows, columns)
    sizes = pltpu.make_async_copy(sizes_hbm, sizes_ref, small)
    sizes.start()
    loads = [
        pltpu.make_async_copy(wave_hbm.at[k], wave_ref.at[k], large.at[k]) for k in range(blocks)
    ]
    for load in loads:
        load.start()
    sizes.wait()
    for k, load in enumerate(loads):
        load.wait()
        keep = inside(sizes_ref[k, 0], shape, 0) & inside(sizes_ref[k, 1], shape, 1)
        masked_ref[k] = jnp.where(keep, wave_ref[k], 0.0)


def own_kernel(
    sizes_hbm, coeff_hbm, source_hbm, masked_ref, left_hbm, right_hbm,
    total_ref, left_high, left_low, right_high, right_low, list_ref,
    sizes_ref, coeff_ref, source_ref, left_ref, right_ref, small, large,
):
    pairs = [(sizes_hbm, sizes_ref), (coeff_hbm, coeff_ref), (source_hbm, source_ref)]
    copies = [pltpu.make_async_copy(*pair, small.at[i]) for i, pair in enumerate(pairs)]
    for copy in copies:
        copy.start()
    terms, blocks, rows, columns = left_ref.shape
    loads = {}
    for k in range(blocks):
        for w in range(terms):
            at = (w, k)
            loads[at] = (
                pltpu.make_async_copy(left_hbm.at[at], left_ref.at[at], large.at[0, w, k]),
                pltpu.make_async_copy(right_hbm.at[at], right_ref.at[at], large.at[1, w, k]),
            )
            for load in loads[at]:
                load.start()
    parts, _, part, _ = total_ref.shape
    shape = (rows, columns)
    total_ref[...] = jnp.zeros_like(total_ref)
    for copy in copies:
        copy.wait()
    first = lax.axis_index("sec") * blocks
    for k in range(blocks):
        count = jnp.int32(0)
        for w in range(terms):
            place = source_ref[k, w] - first
            mine = (place >= 0) & (place < blocks)
            for load in loads[w, k]:
                load.wait()
            scaled = left_ref[w, k] * coeff_ref[k, w]
            left = split(jnp.where(inside(sizes_ref[k, 0], shape, 0), scaled, 0.0))
            right = split(jnp.where(inside(sizes_ref[k, 1], shape, 0), right_ref[w, k], 0.0))

            @pl.when(mine)
            def _():
                chosen = masked_ref[jnp.clip(place, 0, blocks - 1)]
                done = product(left, split(chosen), 0)
                term = product(split(done), right, 1)
                total_ref[:, k] += term.reshape(parts, part, columns)

            @pl.when(~mine)
            def _(count=count):
                list_ref[k, count] = w
                list_ref[k, terms + count] = jnp.where(place < 0, place + blocks, place)
                left_high[w, k], left_low[w, k] = left
                right_high[w, k], right_low[w, k] = right

            count = count + jnp.where(mine, 0, 1)
        list_ref[k, 2 * terms] = count


def other_kernel(
    list_ref, after_ref, before_ref, left_high, left_low, right_high, right_low, sum_ref,
    total_ref, high_ref, low_ref,
):
    terms, blocks, rows, columns = left_high.shape
    parts, _, part, _ = total_ref.shape
    for i in range(2 * blocks):
        value = before_ref[i] if i < blocks else after_ref[i - blocks]
        high_ref[i], low_ref[i] = split(value)
    total_ref[...] = sum_ref[...]
    counts = [list_ref[k, 2 * terms] for k in range(blocks)]
    both = functools.reduce(jnp.minimum, counts)

    def term(k, j):
        w = jnp.clip(list_ref[k, j], 0, terms - 1)
        i = jnp.clip(list_ref[k, terms + j], 0, 2 * blocks - 1)
        done = product((left_high[w, k], left_low[w, k]), (high_ref[i], low_ref[i]), 0)
        return product(split(done), (right_high[w, k], right_low[w, k]), 1)

    for j in range(terms):

        @pl.when(j < both)
        def _():
            results = [term(k, j) for k in range(blocks)]
            for k in range(blocks):
                total_ref[:, k] += results[k].reshape(parts, part, columns)

        for k in range(blocks):

            @pl.when((j >= both) & (j < counts[k]))
            def _():
                total_ref[:, k] += term(k, j).reshape(parts, part, columns)


def on_device(wavefunction, sector_sizes, left_env, right_env, mpo_coeffs, source_block):
    blocks, rows, columns = wavefunction.shape
    terms = left_env.shape[0]
    devices, parts = lax.axis_size("sec"), lax.axis_size("mpo")
    coeffs, sources = mpo_coeffs.T, source_block.T
    params = pltpu.CompilerParams(vmem_limit_bytes=VMEM_LIMIT)
    share = jax.ShapeDtypeStruct((parts, blocks, rows // parts, columns), jnp.float32)
    half = jax.ShapeDtypeStruct((terms, blocks, rows, columns), jnp.bfloat16)
    up = [(i, i + 1) for i in range(devices - 1)]
    down = [(j, i) for i, j in up]

    cost = pl.CostEstimate(flops=10**10, bytes_accessed=1, transcendentals=0)

    masked = pl.pallas_call(
        mask_kernel,
        out_shape=pltpu.VMEM(wavefunction.shape, jnp.float32),
        in_specs=[hbm, hbm],
        out_specs=vmem,
        scratch_shapes=[
            pltpu.SMEM(sector_sizes.shape, jnp.int32),
            pltpu.VMEM(wavefunction.shape, jnp.float32),
            pltpu.SemaphoreType.DMA,
            pltpu.SemaphoreType.DMA((blocks,)),
        ],
        cost_estimate=cost,
        name="mask",
    )(sector_sizes, wavefunction)

    before = lax.ppermute(masked, "sec", up)
    after = lax.ppermute(masked, "sec", down)

    total, *halves, others = pl.pallas_call(
        own_kernel,
        out_shape=[share] + [half] * 4 + [jax.ShapeDtypeStruct((blocks, 8), jnp.int32)],
        in_specs=[hbm] * 3 + [vmem] + [hbm] * 2,
        out_specs=[vmem] * 5 + [smem],
        scratch_shapes=[
            pltpu.SMEM(sector_sizes.shape, jnp.int32),
            pltpu.SMEM(coeffs.shape, jnp.float32),
            pltpu.SMEM(sources.shape, jnp.int32),
            pltpu.VMEM(left_env.shape, jnp.float32),
            pltpu.VMEM(right_env.shape, jnp.float32),
            pltpu.SemaphoreType.DMA((3,)),
            pltpu.SemaphoreType.DMA((2, terms, blocks)),
        ],
        compiler_params=params,
        cost_estimate=cost,
        name="own_terms",
    )(sector_sizes, coeffs, sources, masked, left_env, right_env)

    total = pl.pallas_call(
        other_kernel,
        out_shape=share,
        in_specs=[smem] + [vmem] * 7,
        out_specs=vmem,
        scratch_shapes=[pltpu.VMEM((2 * blocks, rows, columns), jnp.bfloat16)] * 2,
        compiler_params=params,
        cost_estimate=cost,
        name="other_terms",
    )(others, after, before, *halves, total)

    shares = lax.all_to_all(total, "mpo", split_axis=0, concat_axis=0, tiled=True)
    return shares.sum(0)


def solution(mesh):
    in_specs = (
        P("sec", None, None),
        P("sec", None),
        P("mpo", "sec", None, None),
        P("mpo", "sec", None, None),
        P("mpo", "sec"),
        P("mpo", "sec"),
    )
    out_specs = P("sec", "mpo", None)
    return jax.shard_map(
        on_device, mesh=mesh, in_specs=in_specs, out_specs=out_specs, check_vma=False
    )
```

```python
import functools

import jax
import jax.numpy as jnp
from jax import lax
from jax.experimental import pallas as pl
from jax.experimental.pallas import tpu as pltpu
from jax.sharding import PartitionSpec as P

VMEM_LIMIT = 40 * 1024 * 1024
vmem = pl.BlockSpec(memory_space=pltpu.VMEM)
smem = pl.BlockSpec(memory_space=pltpu.SMEM)
hbm = pl.BlockSpec(memory_space=pltpu.HBM)


def inside(limit, shape, dim):
    return lax.broadcasted_iota(jnp.int32, shape, dim) < limit


def split(value):
    high = value.astype(jnp.bfloat16)
    return high, (value - high.astype(jnp.float32)).astype(jnp.bfloat16)


def order(parts):
    return [(parts // 2 - x) % parts for x in range(parts)]


def arranged(value, parts):
    part = value.shape[0] // parts
    return jnp.stack([value[x * part : (x + 1) * part] for x in order(parts)])


def product(left, right, contract):
    (left_high, left_low), (right_high, right_low) = left, right
    return lax.dot_general(
        jnp.concatenate([left_high, left_low, left_high], axis=1),
        jnp.concatenate([right_high, right_high, right_low], axis=contract),
        dimension_numbers=(((1,), (contract,)), ((), ())),
        preferred_element_type=jnp.float32,
    )


def mask_kernel(sizes_hbm, wave_hbm, masked_ref, sizes_ref, wave_ref, small, large):
    blocks, rows, columns = wave_ref.shape
    shape = (rows, columns)
    sizes = pltpu.make_async_copy(sizes_hbm, sizes_ref, small)
    sizes.start()
    loads = [
        pltpu.make_async_copy(wave_hbm.at[k], wave_ref.at[k], large.at[k]) for k in range(blocks)
    ]
    for load in loads:
        load.start()
    sizes.wait()
    for k, load in enumerate(loads):
        load.wait()
        keep = inside(sizes_ref[k, 0], shape, 0) & inside(sizes_ref[k, 1], shape, 1)
        masked_ref[k] = jnp.where(keep, wave_ref[k], 0.0)


def own_kernel(
    sizes_hbm, coeff_hbm, source_hbm, masked_ref, left_hbm, right_hbm,
    total_ref, left_high, left_low, right_high, right_low, list_ref,
    sizes_ref, coeff_ref, source_ref, left_ref, right_ref, small, large,
):
    pairs = [(sizes_hbm, sizes_ref), (coeff_hbm, coeff_ref), (source_hbm, source_ref)]
    copies = [pltpu.make_async_copy(*pair, small.at[i]) for i, pair in enumerate(pairs)]
    for copy in copies:
        copy.start()
    terms, blocks, rows, columns = left_ref.shape
    loads = {}
    for k in range(blocks):
        for w in range(terms):
            at = (w, k)
            loads[at] = (
                pltpu.make_async_copy(left_hbm.at[at], left_ref.at[at], large.at[0, w, k]),
                pltpu.make_async_copy(right_hbm.at[at], right_ref.at[at], large.at[1, w, k]),
            )
            for load in loads[at]:
                load.start()
    parts, _, part, _ = total_ref.shape
    shape = (rows, columns)
    total_ref[...] = jnp.zeros_like(total_ref)
    for copy in copies:
        copy.wait()
    first = lax.axis_index("sec") * blocks
    for k in range(blocks):
        count = jnp.int32(0)
        for w in range(terms):
            place = source_ref[k, w] - first
            mine = (place >= 0) & (place < blocks)
            for load in loads[w, k]:
                load.wait()
            scaled = left_ref[w, k] * coeff_ref[k, w]
            left = split(jnp.where(inside(sizes_ref[k, 0], shape, 0), scaled, 0.0))
            right = split(jnp.where(inside(sizes_ref[k, 1], shape, 0), right_ref[w, k], 0.0))

            @pl.when(mine)
            def _():
                chosen = masked_ref[jnp.clip(place, 0, blocks - 1)]
                done = product(left, split(chosen), 0)
                term = product(split(done), right, 1)
                total_ref[:, k] += arranged(term, parts)

            @pl.when(~mine)
            def _(count=count):
                list_ref[k, count] = w
                list_ref[k, terms + count] = jnp.where(place < 0, place + blocks, place)
                left_high[w, k], left_low[w, k] = left
                right_high[w, k], right_low[w, k] = right

            count = count + jnp.where(mine, 0, 1)
        list_ref[k, 2 * terms] = count


def other_kernel(
    list_ref, after_ref, before_ref, left_high, left_low, right_high, right_low, sum_ref,
    total_ref, high_ref, low_ref,
):
    terms, blocks, rows, columns = left_high.shape
    parts, _, part, _ = total_ref.shape
    for i in range(2 * blocks):
        value = before_ref[i] if i < blocks else after_ref[i - blocks]
        high_ref[i], low_ref[i] = split(value)
    counts = [list_ref[k, 2 * terms] for k in range(blocks)]
    both = functools.reduce(jnp.minimum, counts)

    def first_product(k, j):
        w = jnp.clip(list_ref[k, j], 0, terms - 1)
        i = jnp.clip(list_ref[k, terms + j], 0, 2 * blocks - 1)
        done = product((left_high[w, k], left_low[w, k]), (high_ref[i], low_ref[i]), 0)
        return split(done), (right_high[w, k], right_low[w, k])

    def sum_of_terms(k, places):
        pairs = [first_product(k, j) for j in places]
        left, right = (
            tuple(jnp.concatenate([pair[side][part] for pair in pairs], axis=1) for part in (0, 1))
            for side in (0, 1)
        )
        return arranged(product(left, right, 1), parts)

    @pl.when(both >= 2)
    def _():
        for k in range(blocks):
            total_ref[:, k] = sum_ref[:, k] + sum_of_terms(k, (0, 1))

    @pl.when(both < 2)
    def _():
        total_ref[...] = sum_ref[...]
        for k in range(blocks):
            for j in range(min(2, terms)):

                @pl.when(j < counts[k])
                def _():
                    total_ref[:, k] += sum_of_terms(k, (j,))

    for j in range(2, terms):
        for k in range(blocks):

            @pl.when(j < counts[k])
            def _():
                total_ref[:, k] += sum_of_terms(k, (j,))


def on_device(wavefunction, sector_sizes, left_env, right_env, mpo_coeffs, source_block):
    blocks, rows, columns = wavefunction.shape
    terms = left_env.shape[0]
    devices, parts = lax.axis_size("sec"), lax.axis_size("mpo")
    coeffs, sources = mpo_coeffs.T, source_block.T
    params = pltpu.CompilerParams(vmem_limit_bytes=VMEM_LIMIT)
    share = jax.ShapeDtypeStruct((parts, blocks, rows // parts, columns), jnp.float32)
    half = jax.ShapeDtypeStruct((terms, blocks, rows, columns), jnp.bfloat16)
    up = [(i, i + 1) for i in range(devices - 1)]
    down = [(j, i) for i, j in up]

    cost = pl.CostEstimate(flops=10**10, bytes_accessed=1, transcendentals=0)

    masked = pl.pallas_call(
        mask_kernel,
        out_shape=pltpu.VMEM(wavefunction.shape, jnp.float32),
        in_specs=[hbm, hbm],
        out_specs=vmem,
        scratch_shapes=[
            pltpu.SMEM(sector_sizes.shape, jnp.int32),
            pltpu.VMEM(wavefunction.shape, jnp.float32),
            pltpu.SemaphoreType.DMA,
            pltpu.SemaphoreType.DMA((blocks,)),
        ],
        cost_estimate=cost,
        name="mask",
    )(sector_sizes, wavefunction)

    before = lax.ppermute(masked, "sec", up)
    after = lax.ppermute(masked, "sec", down)

    total, *halves, others = pl.pallas_call(
        own_kernel,
        out_shape=[share] + [half] * 4 + [jax.ShapeDtypeStruct((blocks, 8), jnp.int32)],
        in_specs=[hbm] * 3 + [vmem] + [hbm] * 2,
        out_specs=[vmem] * 5 + [smem],
        scratch_shapes=[
            pltpu.SMEM(sector_sizes.shape, jnp.int32),
            pltpu.SMEM(coeffs.shape, jnp.float32),
            pltpu.SMEM(sources.shape, jnp.int32),
            pltpu.VMEM(left_env.shape, jnp.float32),
            pltpu.VMEM(right_env.shape, jnp.float32),
            pltpu.SemaphoreType.DMA((3,)),
            pltpu.SemaphoreType.DMA((2, terms, blocks)),
        ],
        compiler_params=params,
        cost_estimate=cost,
        name="own_terms",
    )(sector_sizes, coeffs, sources, masked, left_env, right_env)

    total = pl.pallas_call(
        other_kernel,
        out_shape=share,
        in_specs=[smem] + [vmem] * 7,
        out_specs=vmem,
        scratch_shapes=[pltpu.VMEM((2 * blocks, rows, columns), jnp.bfloat16)] * 2,
        compiler_params=params,
        cost_estimate=cost,
        name="other_terms",
    )(others, after, before, *halves, total)

    shares = lax.all_to_all(total, "mpo", split_axis=0, concat_axis=0, tiled=True, axis_index_groups=[order(parts)])
    return shares.sum(0)


def solution(mesh):
    in_specs = (
        P("sec", None, None),
        P("sec", None),
        P("mpo", "sec", None, None),
        P("mpo", "sec", None, None),
        P("mpo", "sec"),
        P("mpo", "sec"),
    )
    out_specs = P("sec", "mpo", None)
    return jax.shard_map(
        on_device, mesh=mesh, in_specs=in_specs, out_specs=out_specs, check_vma=False
    )
```

```python
import functools

import jax
import jax.numpy as jnp
from jax import lax
from jax.experimental import pallas as pl
from jax.experimental.pallas import tpu as pltpu
from jax.sharding import PartitionSpec as P

VMEM_LIMIT = 40 * 1024 * 1024
vmem = pl.BlockSpec(memory_space=pltpu.VMEM)
smem = pl.BlockSpec(memory_space=pltpu.SMEM)
hbm = pl.BlockSpec(memory_space=pltpu.HBM)


def inside(limit, shape, dim):
    return lax.broadcasted_iota(jnp.int32, shape, dim) < limit


def split(value):
    high = value.astype(jnp.bfloat16)
    return high, (value - high.astype(jnp.float32)).astype(jnp.bfloat16)


def order(parts):
    return [(parts // 2 - x) % parts for x in range(parts)]


def arranged(value, parts):
    part = value.shape[0] // parts
    return jnp.stack([value[x * part : (x + 1) * part] for x in order(parts)])


def product(left, right, contract):
    (left_high, left_low), (right_high, right_low) = left, right
    return lax.dot_general(
        jnp.concatenate([left_high, left_low, left_high], axis=1),
        jnp.concatenate([right_high, right_high, right_low], axis=contract),
        dimension_numbers=(((1,), (contract,)), ((), ())),
        preferred_element_type=jnp.float32,
    )


def mask_kernel(sizes_hbm, wave_hbm, masked_ref, sizes_ref, wave_ref, small, large):
    blocks, rows, columns = wave_ref.shape
    shape = (rows, columns)
    sizes = pltpu.make_async_copy(sizes_hbm, sizes_ref, small)
    sizes.start()
    loads = [
        pltpu.make_async_copy(wave_hbm.at[k], wave_ref.at[k], large.at[k]) for k in range(blocks)
    ]
    for load in loads:
        load.start()
    sizes.wait()
    for k, load in enumerate(loads):
        load.wait()
        keep = inside(sizes_ref[k, 0], shape, 0) & inside(sizes_ref[k, 1], shape, 1)
        masked_ref[k] = jnp.where(keep, wave_ref[k], 0.0)


def own_kernel(
    sizes_hbm, coeff_hbm, source_hbm, masked_ref, left_hbm, right_hbm,
    total_ref, left_high, left_low, right_high, right_low, list_ref,
    sizes_ref, coeff_ref, source_ref, left_ref, right_ref, small, large,
):
    pairs = [(sizes_hbm, sizes_ref), (coeff_hbm, coeff_ref), (source_hbm, source_ref)]
    copies = [pltpu.make_async_copy(*pair, small.at[i]) for i, pair in enumerate(pairs)]
    for copy in copies:
        copy.start()
    terms, blocks, rows, columns = left_ref.shape
    loads = {}
    for k in range(blocks):
        for w in range(terms):
            at = (w, k)
            loads[at] = (
                pltpu.make_async_copy(left_hbm.at[at], left_ref.at[at], large.at[0, w, k]),
                pltpu.make_async_copy(right_hbm.at[at], right_ref.at[at], large.at[1, w, k]),
            )
            for load in loads[at]:
                load.start()
    parts, _, part, _ = total_ref.shape
    shape = (rows, columns)
    total_ref[...] = jnp.zeros_like(total_ref)
    for copy in copies:
        copy.wait()
    first = lax.axis_index("sec") * blocks
    for k in range(blocks):
        counts = [jnp.int32(0), jnp.int32(0)]
        for w in range(terms):
            place = source_ref[k, w] - first
            mine = (place >= 0) & (place < blocks)
            for load in loads[w, k]:
                load.wait()
            scaled = left_ref[w, k] * coeff_ref[k, w]
            left = split(jnp.where(inside(sizes_ref[k, 0], shape, 0), scaled, 0.0))
            right = split(jnp.where(inside(sizes_ref[k, 1], shape, 0), right_ref[w, k], 0.0))

            @pl.when(mine)
            def _():
                chosen = masked_ref[jnp.clip(place, 0, blocks - 1)]
                done = product(left, split(chosen), 0)
                term = product(split(done), right, 1)
                total_ref[:, k] += arranged(term, parts)

            for side, belongs in enumerate((place < 0, place >= blocks)):

                @pl.when(belongs)
                def _(side=side, count=counts[side]):
                    list_ref[k, side * 8 + count] = w
                    list_ref[k, side * 8 + terms + count] = place + blocks * (1 - 2 * side)

                counts[side] = counts[side] + jnp.where(belongs, 1, 0)

            @pl.when(~mine)
            def _():
                left_high[w, k], left_low[w, k] = left
                right_high[w, k], right_low[w, k] = right

        for side in (0, 1):
            list_ref[k, side * 8 + 2 * terms] = counts[side]


def side_kernel(
    side, list_ref, received_ref, left_high, left_low, right_high, right_low, sum_ref,
    total_ref, high_ref, low_ref,
):
    terms, blocks, rows, columns = left_high.shape
    parts = total_ref.shape[0]
    base = side * 8
    for i in range(blocks):
        high_ref[i], low_ref[i] = split(received_ref[i])
    counts = [list_ref[k, base + 2 * terms] for k in range(blocks)]
    both = functools.reduce(jnp.minimum, counts)

    def term(k, j):
        w = jnp.clip(list_ref[k, base + j], 0, terms - 1)
        i = jnp.clip(list_ref[k, base + terms + j], 0, blocks - 1)
        done = product((left_high[w, k], left_low[w, k]), (high_ref[i], low_ref[i]), 0)
        return arranged(product(split(done), (right_high[w, k], right_low[w, k]), 1), parts)

    @pl.when(both >= 1)
    def _():
        for k in range(blocks):
            total_ref[:, k] = sum_ref[:, k] + term(k, 0)

    @pl.when(both < 1)
    def _():
        total_ref[...] = sum_ref[...]
        for k in range(blocks):

            @pl.when(counts[k] > 0)
            def _():
                total_ref[:, k] += term(k, 0)

    for j in range(1, terms):
        for k in range(blocks):

            @pl.when(j < counts[k])
            def _():
                total_ref[:, k] += term(k, j)


def on_device(wavefunction, sector_sizes, left_env, right_env, mpo_coeffs, source_block):
    blocks, rows, columns = wavefunction.shape
    terms = left_env.shape[0]
    devices, parts = lax.axis_size("sec"), lax.axis_size("mpo")
    coeffs, sources = mpo_coeffs.T, source_block.T
    params = pltpu.CompilerParams(vmem_limit_bytes=VMEM_LIMIT)
    share = jax.ShapeDtypeStruct((parts, blocks, rows // parts, columns), jnp.float32)
    half = jax.ShapeDtypeStruct((terms, blocks, rows, columns), jnp.bfloat16)
    up = [(i, i + 1) for i in range(devices - 1)]
    down = [(j, i) for i, j in up]

    cost = pl.CostEstimate(flops=10**10, bytes_accessed=1, transcendentals=0)

    masked = pl.pallas_call(
        mask_kernel,
        out_shape=pltpu.VMEM(wavefunction.shape, jnp.float32),
        in_specs=[hbm, hbm],
        out_specs=vmem,
        scratch_shapes=[
            pltpu.SMEM(sector_sizes.shape, jnp.int32),
            pltpu.VMEM(wavefunction.shape, jnp.float32),
            pltpu.SemaphoreType.DMA,
            pltpu.SemaphoreType.DMA((blocks,)),
        ],
        cost_estimate=cost,
        name="mask",
    )(sector_sizes, wavefunction)

    before = lax.ppermute(masked, "sec", up)
    after = lax.ppermute(masked, "sec", down)

    total, *halves, others = pl.pallas_call(
        own_kernel,
        out_shape=[share] + [half] * 4 + [jax.ShapeDtypeStruct((blocks, 16), jnp.int32)],
        in_specs=[hbm] * 3 + [vmem] + [hbm] * 2,
        out_specs=[vmem] * 5 + [smem],
        scratch_shapes=[
            pltpu.SMEM(sector_sizes.shape, jnp.int32),
            pltpu.SMEM(coeffs.shape, jnp.float32),
            pltpu.SMEM(sources.shape, jnp.int32),
            pltpu.VMEM(left_env.shape, jnp.float32),
            pltpu.VMEM(right_env.shape, jnp.float32),
            pltpu.SemaphoreType.DMA((3,)),
            pltpu.SemaphoreType.DMA((2, terms, blocks)),
        ],
        compiler_params=params,
        cost_estimate=cost,
        name="own_terms",
    )(sector_sizes, coeffs, sources, masked, left_env, right_env)

    for side, received in enumerate((before, after)):
        total = pl.pallas_call(
            functools.partial(side_kernel, side),
            out_shape=pltpu.VMEM(share.shape, jnp.float32),
            in_specs=[smem] + [vmem] * 6,
            out_specs=vmem,
            scratch_shapes=[pltpu.VMEM((blocks, rows, columns), jnp.bfloat16)] * 2,
            compiler_params=params,
            cost_estimate=cost,
            name=("before_terms", "after_terms")[side],
        )(others, received, *halves, total)

    shares = lax.all_to_all(total, "mpo", split_axis=0, concat_axis=0, tiled=True, axis_index_groups=[order(parts)])
    return shares.sum(0)


def solution(mesh):
    in_specs = (
        P("sec", None, None),
        P("sec", None),
        P("mpo", "sec", None, None),
        P("mpo", "sec", None, None),
        P("mpo", "sec"),
        P("mpo", "sec"),
    )
    out_specs = P("sec", "mpo", None)
    return jax.shard_map(
        on_device, mesh=mesh, in_specs=in_specs, out_specs=out_specs, check_vma=False
    )
```
